512 devices in a mesh: row: 32 (over x, y_hi, core), col: 16 (over z, y_lo).
Axes of the slice: x: 4, y: 8 (y_hi: 4, y_lo: 2; y = y_hi * 2 + y_lo), z: 8, core: 2. Of those that a mesh axis runs over, the one named last changes fastest.
Arguments:
- tokens: bfloat16 [8192, 3072], P('row', 'col'), may hold values from -6 to 6
- w_in: bfloat16 [3072, 12288], P('row', 'col'), may hold values from -0.109375 to 0.109375
- w_out: bfloat16 [12288, 3072], P('row', 'col'), may hold values from -0.0546875 to 0.0546875
Outputs:
- mixed: bfloat16 [8192, 3072], P('row', 'col')
The draws below stay inside these ranges and needn't reach their ends.
All inputs are finite; a program needn't handle non-finite values.
Results may differ from the reference program's by a relative error of at most 0.0049.
Values may be sent and summed in bfloat16 or wider, within the bound.
A program may use at most 64 MiB of HBM per device.

```python
import jax
import jax.numpy as jnp

D = 3072
FF = 12288
TOKENS = 8192


def levels(own_key, dims, cuts, least, largest):
    def one(axis_at, shards_of):
        steps = jax.random.uniform(jax.random.fold_in(jax.random.fold_in(own_key, 6), axis_at), (shards_of,), jnp.float32, least / len(cuts), largest / len(cuts))
        return jnp.repeat(jnp.exp(steps), dims[axis_at] // shards_of).reshape((-1,) + (1,) * (len(dims) - axis_at - 1))

    gain = one(*cuts[0])
    for cut in cuts[1:]:
        gain = gain * one(*cut)
    return gain


def noise(stream_key, extent, scale, most, pieces=(), kind=jnp.bfloat16):
    level = levels(stream_key, extent, pieces, -0.22, 0.18) if pieces else 1.0
    drawn = jax.random.normal(stream_key, extent, jnp.float32) * scale * level
    return jnp.minimum(jnp.maximum(drawn, -most), most).astype(kind)


def setup_inputs(seed: int = 0) -> dict:
    seeds = jax.random.split(jax.random.key(seed), 4)
    tokens = noise(seeds[0], (TOKENS, D), 1.0, 6.0, ((0, 32), (1, 16)))
    w_in = noise(seeds[1], (D, FF), D ** -0.5, 0.109375, ((0, 32), (1, 16)))
    w_out = noise(seeds[2], (FF, D), FF ** -0.5, 0.0546875, ((0, 32), (1, 16)))
    return dict(tokens=tokens, w_in=w_in, w_out=w_out)


def reference(tokens, w_in, w_out):
    pre = jnp.dot(tokens, w_in, preferred_element_type=jnp.float32)
    hidden = jax.nn.gelu(pre, approximate=False).astype(jnp.bfloat16)
    return jnp.dot(hidden, w_out, preferred_element_type=jnp.float32).astype(jnp.bfloat16)
```

```python
import jax
import jax.numpy as jnp
from jax import lax
from jax.experimental import pallas as pl
from jax.experimental.pallas import tpu as pltpu
from jax.sharding import PartitionSpec as P

MESH = pl.DeviceIdType.MESH
BF16, F32 = jnp.bfloat16, jnp.float32
SEMS = 128


def horner(v, terms):
    total = jnp.full_like(v, terms[0])
    for term in terms[1:]:
        total = total * v + term
    return total


ERF_NEAR = (7.853861353153693e-5, -8.010193625184903e-4, 5.188327685732524e-3, -2.685381193529856e-2,
            1.128358514861418e-1, -3.761262582423300e-1, 1.128379165726710e0)
ERFC_MID = (2.326819970068386e-2, -1.387039388740657e-1, 3.687424674597105e-1, -5.824733027278666e-1,
            6.210004621745983e-1, -4.944515323274145e-1, 3.404879937665872e-1, -2.741127028184656e-1,
            5.638259427386472e-1)
ERFC_FAR = (-1.047766399936249e1, 1.297719955372516e1, -7.495518717768503e0, 2.921019019210786e0,
            -1.015265279202700e0, 4.218463358204948e-1, -2.820767439740514e-1, 5.641895067754075e-1)


def gelu(v):
    u = v * (-(0.5**0.5))
    square = u * u
    size = jnp.maximum(jnp.abs(u), 0.5)
    near = 1.0 - u * horner(jnp.minimum(square, 1.0), ERF_NEAR)
    inverse = 1.0 / size
    y = inverse * inverse
    series = jnp.where(size < 2.0, horner(jnp.minimum(y, 1.0), ERFC_MID), horner(jnp.minimum(y, 0.25), ERFC_FAR))
    tail = jnp.exp(-square) * inverse * series
    far = jnp.where(u < 0.0, 2.0 - tail, tail)
    return 0.5 * v * jnp.where(jnp.abs(u) < 1.0, near, far)


def kernel(tok_ref, win_ref, wout_ref, out_ref, tk, wi, wo, tokp, woh, wop, hid, acc, part, rs_out, rs_in, end_out, end_in,
           send_sem, recv_sem, local_sem):
    r, c = lax.axis_index("row"), lax.axis_index("col")
    x, yh, p, z, yl = r // 8, (r // 2) % 4, r % 2, c // 2, c % 2

    def device(x, yh, p, z, yl):
        return ((x % 4) * 8 + (yh % 4) * 2 + p, (z % 8) * 2 + yl)

    right, left = device(x + 1, yh, p, z, yl), device(x + 3, yh, p, z, yl)
    far_y, near_y = device(x, yh + 1, p, z, yl), device(x, yh + 3, p, z, yl)
    up, down = device(x, yh, p, z + 1, yl), device(x, yh, p, z + 7, yl)
    pair, sibling = device(x, yh, p, z, 1 - yl), device(x, yh, 1 - p, z, yl)

    flip = (yh // 2 + z) % 2
    other_x = (z // 2 + 4 - x) % 4
    spread = [device(other_x, 2 * flip + half, p, z, yh % 2) for half in range(2)]
    spread_from = [device(other_x, 2 * flip + yl, p, z, half) for half in range(2)]
    lift = device(x, yh, p, 2 * other_x + flip, yl)
    lift_from = device(x, yh, p, 2 * ((z // 2 + x) % 4) + flip, yl)

    sems = [0]
    started = []

    def copy(src, dst, to, mark=None):
        k = sems[0]
        sems[0] += 1
        mark = k if mark is None else mark
        return pltpu.make_async_remote_copy(
            src_ref=src, dst_ref=dst, send_sem=send_sem.at[k], recv_sem=recv_sem.at[mark], device_id=to, device_id_type=MESH
        )

    def send(src, dst, to):
        made = copy(src, dst, to)
        made.start()
        started.append(made)
        return made

    def send_maybe(src, dst, to, mark=None):
        mark = sems[0] if mark is None else mark
        made = copy(src, dst, to, mark)
        here = jnp.logical_and(to[0] == r, to[1] == c)

        @pl.when(here)
        def _():
            pltpu.make_async_copy(src, dst, recv_sem.at[mark]).start()

        @pl.when(jnp.logical_not(here))
        def _():
            made.start()

        def end():
            @pl.when(jnp.logical_not(here))
            def _():
                made.wait_send()

        return made, end

    def w1(dx, dy, core, half=None):
        px, py = (x + dx) % 4, (yh + dy) % 4
        at = wi.at[2 * px + py // 2, py % 2, core]
        return at if half is None else at.at[pl.ds(48 * half, 48)]

    def w1_group(dx, core):
        return wi.at[pl.ds(2 * ((x + dx) % 4), 2), :, core]

    def w2(dx, dy, core, half=None):
        px, py = (x + dx) % 4, (yh + dy) % 4
        at = wo.at[2 * ((z // 2 + px) % 4) + (z + py // 2) % 2, core, py % 2]
        return at if half is None else at.at[pl.ds(96 * half, 96)]

    def w2_group(dx, core):
        return wo.at[pl.ds(2 * ((z // 2 + x + dx) % 4), 2), core]

    barrier = pltpu.get_barrier_semaphore()
    greeted = [right, left, far_y, near_y, up, down, pair, sibling, *spread_from, lift_from]
    for to in greeted:
        pl.semaphore_signal(barrier, inc=1, device_id=to, device_id_type=MESH)
    pl.semaphore_wait(barrier, len(greeted))

    own_w1 = pltpu.make_async_copy(win_ref, w1(0, 0, p), local_sem.at[0])
    own_tok = pltpu.make_async_copy(tok_ref, tokp.at[yl], local_sem.at[1])
    own_w1.start()
    own_tok.start()
    tok_pair = send(tok_ref, tokp.at[yl], pair)
    y1 = {d: send(win_ref, w1(0, 0, p), to) for d, to in ((-1, far_y), (1, near_y))}
    halves = [
        send_maybe(wout_ref.at[pl.ds(192 * half, 192)], woh.at[yl], spread[half], SEMS + yl) for half in range(2)
    ]

    class Gather:
        def __init__(self, at, group):
            self.at, self.group = at, group
            self.x, self.xh, self.yh, self.sib = {}, {}, {}, {}

        def y_own(self, src):
            self.y = {d: send(src, self.at(0, 0, p), to) for d, to in ((-1, far_y), (1, near_y))}

        def y_forward(self):
            self.y[-1].wait_recv()
            self.yh[0] = send(self.at(0, -1, p, 0), self.at(0, -1, p, 0), far_y)
            self.x_send(-1)
            self.y[1].wait_recv()
            self.yh[1] = send(self.at(0, 1, p, 1), self.at(0, 1, p, 1), near_y)
            self.x_send(1)

        def y_last(self):
            self.yh[0].wait_recv()
            self.yh[1].wait_recv()
            self.x_send(2)

        def x_send(self, dy, src=None):
            src = self.at(0, dy, p) if src is None else src
            for d, to in ((-1, right), (1, left)):
                self.x[d, dy] = send(src, self.at(0, dy, p), to)

        def x_forward(self, dy):
            self.x[-1, dy].wait_recv()
            self.xh[0, dy] = send(self.at(-1, dy, p, 0), self.at(-1, dy, p, 0), right)
            self.x[1, dy].wait_recv()
            self.xh[1, dy] = send(self.at(1, dy, p, 1), self.at(1, dy, p, 1), left)

        def x_last(self):
            for made in self.xh.values():
                made.wait_recv()

        def share(self, dx):
            self.sib[dx] = send(self.group(dx, p), self.group(dx, p), sibling)

    first, second = Gather(w1, w1_group), Gather(w2, w2_group)
    first.y = y1
    first.x_send(0, win_ref)

    tok_pair.wait_recv()
    own_tok.wait()
    tk[z] = jnp.concatenate([tokp[0], tokp[1]], axis=1)
    ring = {}
    ring[0, 0] = send(tk.at[z], tk.at[z], up)
    ring[1, 0] = send(tk.at[z], tk.at[z], down)

    for half in range(2):
        pltpu.make_async_copy(woh.at[half], woh.at[half], recv_sem.at[SEMS + half]).wait()
    wop[...] = jnp.concatenate([woh[0], woh[1]], axis=1)
    lifted, lift_end = send_maybe(wop, wo.at[z, p, yh % 2], lift)

    def ring_step(step):
        for way, to in ((0, up), (1, down)):
            ring[way, step - 1].wait_recv()
            at = tk.at[(z + 8 - step) % 8 if way == 0 else (z + step) % 8]
            if step == 3:
                at = at.at[pl.ds(128 * way, 128)]
            ring[way, step] = send(at, at, to)

    ring_step(1)
    first.x_forward(0)
    first.y_forward()
    ring_step(2)
    first.x_forward(-1)
    first.x_forward(1)
    first.y_last()
    own_w1.wait()
    first.share(0)
    ring_step(3)
    lifted.wait_recv()
    second.y_own(w2(0, 0, p))
    first.x_forward(2)
    first.share(-1)
    first.share(1)
    second.x_send(0)
    ring[0, 3].wait_recv()
    ring[1, 3].wait_recv()

    def product(dx):
        first.sib[dx].wait_recv()
        total = None
        for k in range(2):
            at = 2 * ((x + dx) % 4) + k
            new = jnp.dot(tk[at], wi[at].reshape(384, 768), preferred_element_type=F32)
            total = new if total is None else total + new
        return total

    acc[...] = product(0)
    second.y_forward()
    acc[...] += product(-1)
    second.x_forward(0)
    acc[...] += product(1)
    first.x_last()
    first.share(2)
    second.y_last()
    second.share(0)
    acc[...] += product(2)

    @pl.loop(0, 16)
    def _(i):
        rows = pl.ds(pl.multiple_of(i * 16, 16), 16)
        hid[rows] = gelu(acc[rows]).astype(BF16)

    second.x_forward(-1)
    second.x_forward(1)
    second.x_forward(2)
    second.share(-1)
    second.share(1)
    second.x_last()
    second.share(2)
    for dx in (0, -1, 1, 2):
        second.sib[dx].wait_recv()

    place = {4: 0, 3: 1, -3: 2, 2: 3, -2: 4, 1: 5, -1: 6, 0: 7}

    def partial(distance):
        weights = wo[(z + 8 + distance) % 8].reshape(768, 384)
        part[place[distance]] = jnp.dot(hid[...], weights, preferred_element_type=F32)

    moved = {}

    def pass_on(name, k, distance):
        for way, to in ((0, up), (1, down)):
            low = (way == 0) == (name == "a")
            rows = slice(0, 128) if low else slice(128, 256)
            value = part[place[distance if way == 0 or distance == 4 else -distance], rows]
            slot = 2 * k if name == "a" else 2 * k + 1
            if k:
                moved[way, name, k - 1].wait_recv()
                value = value + rs_in[way, slot - 2].astype(F32)
            rs_out[way, slot] = value.astype(BF16)
            moved[way, name, k] = send(rs_out.at[way, slot], rs_in.at[way, slot], to)

    partial(4)
    pass_on("a", 0, 4)
    partial(3)
    partial(-3)
    pass_on("b", 0, 3)
    partial(2)
    partial(-2)
    pass_on("a", 1, 3)
    pass_on("b", 1, 2)
    partial(1)
    partial(-1)
    pass_on("a", 2, 2)
    partial(0)
    pass_on("b", 2, 1)
    pass_on("a", 3, 1)
    moved[0, "b", 2].wait_recv()
    moved[1, "b", 2].wait_recv()
    mine = {}
    last = {}
    for half in range(2):
        rows = slice(128 * half, 128 * half + 128)
        moved[half, "a", 3].wait_recv()
        total = part[place[0], rows] + rs_in[half, 6].astype(F32) + rs_in[1 - half, 5].astype(F32)
        low, high = total[:, :192], total[:, 192:]
        end_out[half] = jnp.where(yl == 0, high, low).astype(BF16)
        last[half] = send(end_out.at[half], end_in.at[half], pair)
        part[place[4], rows, :192] = jnp.where(yl == 0, low, high)
    for half in range(2):
        rows = slice(128 * half, 128 * half + 128)
        last[half].wait_recv()
        out_ref[rows] = (part[place[4], rows, :192] + end_in[half].astype(F32)).astype(BF16)

    for made in started:
        made.wait_send()
    halves[0][1]()
    halves[1][1]()
    lift_end()


def local(tokens, w_in, w_out):
    return pl.pallas_call(
        kernel,
        name="mlp_block",
        out_shape=jax.ShapeDtypeStruct((256, 192), BF16),
        in_specs=[pl.BlockSpec(memory_space=pl.ANY)] * 3,
        out_specs=pl.BlockSpec(memory_space=pltpu.VMEM),
        scratch_shapes=[
            pltpu.VMEM((8, 256, 384), BF16),
            pltpu.VMEM((8, 2, 2, 96, 768), BF16),
            pltpu.VMEM((8, 2, 2, 192, 384), BF16),
            pltpu.VMEM((2, 256, 192), BF16),
            pltpu.VMEM((2, 192, 192), BF16),
            pltpu.VMEM((192, 384), BF16),
            pltpu.VMEM((256, 768), BF16),
            pltpu.VMEM((256, 768), F32),
            pltpu.VMEM((8, 256, 384), F32),
            pltpu.VMEM((2, 7, 128, 384), BF16),
            pltpu.VMEM((2, 7, 128, 384), BF16),
            pltpu.VMEM((2, 128, 192), BF16),
            pltpu.VMEM((2, 128, 192), BF16),
            pltpu.SemaphoreType.DMA((SEMS,)),
            pltpu.SemaphoreType.DMA((SEMS + 2,)),
            pltpu.SemaphoreType.DMA((2,)),
        ],
        compiler_params=pltpu.CompilerParams(collective_id=0, has_side_effects=True, vmem_limit_bytes=48 * 2**20),
        cost_estimate=pl.CostEstimate(flops=4 * 256 * 3072 * 768, bytes_accessed=2**20, transcendentals=2**18),
    )(tokens, w_in, w_out)


def solution(mesh):
    placed = (P("row", "col"), P("row", "col"), P("row", "col"))
    return jax.shard_map(local, mesh=mesh, in_specs=placed, out_specs=P("row", "col"), check_vma=False)
```

```python
import jax
import jax.numpy as jnp
from jax import lax
from jax.experimental import pallas as pl
from jax.experimental.pallas import tpu as pltpu
from jax.sharding import PartitionSpec as P

MESH = pl.DeviceIdType.MESH
BF16, F32 = jnp.bfloat16, jnp.float32
SEMS = 92


def horner(v, terms):
    total = jnp.full_like(v, terms[0])
    for term in terms[1:]:
        total = total * v + term
    return total


ERF_NEAR = (7.853861353153693e-5, -8.010193625184903e-4, 5.188327685732524e-3, -2.685381193529856e-2,
            1.128358514861418e-1, -3.761262582423300e-1, 1.128379165726710e0)
ERFC_MID = (2.326819970068386e-2, -1.387039388740657e-1, 3.687424674597105e-1, -5.824733027278666e-1,
            6.210004621745983e-1, -4.944515323274145e-1, 3.404879937665872e-1, -2.741127028184656e-1,
            5.638259427386472e-1)
ERFC_FAR = (-1.047766399936249e1, 1.297719955372516e1, -7.495518717768503e0, 2.921019019210786e0,
            -1.015265279202700e0, 4.218463358204948e-1, -2.820767439740514e-1, 5.641895067754075e-1)


def gelu(v):
    u = v * (-(0.5**0.5))
    square = u * u
    size = jnp.maximum(jnp.abs(u), 0.5)
    near = 1.0 - u * horner(jnp.minimum(square, 1.0), ERF_NEAR)
    inverse = 1.0 / size
    y = inverse * inverse
    series = jnp.where(size < 2.0, horner(jnp.minimum(y, 1.0), ERFC_MID), horner(jnp.minimum(y, 0.25), ERFC_FAR))
    tail = jnp.exp(-square) * inverse * series
    far = jnp.where(u < 0.0, 2.0 - tail, tail)
    return 0.5 * v * jnp.where(jnp.abs(u) < 1.0, near, far)


def kernel(tok_ref, win_ref, wout_ref, out_ref, tk, wi, wo, tokp, stage, hid, acc, part, rs_out, rs_in, swap_out, swap_in,
           send_sem, recv_sem, local_sem):
    r, c = lax.axis_index("row"), lax.axis_index("col")
    x, yh, p, z, yl = r // 8, (r // 2) % 4, r % 2, c // 2, c % 2

    def device(x, yh, p, z, yl):
        return ((x % 4) * 8 + (yh % 4) * 2 + p, (z % 8) * 2 + yl)

    right, left = device(x + 1, yh, p, z, yl), device(x + 3, yh, p, z, yl)
    far_y, near_y = device(x, yh + 1, p, z, yl), device(x, yh + 3, p, z, yl)
    up, down = device(x, yh, p, z + 1, yl), device(x, yh, p, z + 7, yl)
    up_pair, down_pair = device(x, yh, p, z + 1, 1 - yl), device(x, yh, p, z + 7, 1 - yl)
    pair, sibling = device(x, yh, p, z, 1 - yl), device(x, yh, 1 - p, z, yl)

    other_x = (z // 2 + 4 - x) % 4
    spread = device(other_x, 2 * ((yh // 2 + z + yl) % 2) + yl, p, z, yh % 2)
    top = (yh // 2 + z + yh) % 2
    spread_from = device(other_x, 2 * top + yl, p, z, yh % 2)
    lift = device(x, yh, p, 2 * other_x + top, yl)
    lift_from = device(x, yh, p, 2 * ((z // 2 + x) % 4) + top, yl)

    sems = [0]
    started = []

    def copy(src, dst, to):
        k = sems[0]
        sems[0] += 1
        return pltpu.make_async_remote_copy(
            src_ref=src, dst_ref=dst, send_sem=send_sem.at[k], recv_sem=recv_sem.at[k], device_id=to, device_id_type=MESH
        )

    def send(src, dst, to):
        made = copy(src, dst, to)
        made.start()
        started.append(made)
        return made

    def sent(made):
        made.wait_send()
        started[:] = [other for other in started if other is not made]

    def send_maybe(src, dst, to):
        k = sems[0]
        made = copy(src, dst, to)
        here = jnp.logical_and(to[0] == r, to[1] == c)

        @pl.when(here)
        def _():
            pltpu.make_async_copy(src, dst, recv_sem.at[k]).start()

        @pl.when(jnp.logical_not(here))
        def _():
            made.start()

        def end():
            @pl.when(jnp.logical_not(here))
            def _():
                made.wait_send()

        return made, end

    def w1(dx, dy, core, half=None):
        px, py = (x + dx) % 4, (yh + dy) % 4
        at = wi.at[2 * px + py // 2, py % 2, core]
        return at if half is None else at.at[pl.ds(48 * half, 48)]

    def w1_group(dx, core):
        return wi.at[pl.ds(2 * ((x + dx) % 4), 2), :, core]

    def w2(dx, dy, core, half=None):
        px, py = (x + dx) % 4, (yh + dy) % 4
        at = wo.at[2 * ((z // 2 + px) % 4) + (z + py // 2 + py) % 2, core, py % 2]
        return at if half is None else at.at[pl.ds(96 * half, 96)]

    def w2_group(dx, core):
        return wo.at[pl.ds(2 * ((z // 2 + x + dx) % 4), 2), core]

    class Gather:
        def __init__(self, at, group, far):
            self.at, self.group, self.by_y = at, group, far
            self.x, self.xh, self.yh, self.fh, self.sib = {}, {}, {}, {}, {}

        def y_own(self, src):
            self.y = {d: send(src, self.at(0, 0, p), to) for d, to in ((-1, far_y), (1, near_y))}

        def y_forward(self):
            self.y[-1].wait_recv()
            self.yh[0] = send(self.at(0, -1, p, 0), self.at(0, -1, p, 0), far_y)
            self.x_send(-1)
            self.y[1].wait_recv()
            self.yh[1] = send(self.at(0, 1, p, 1), self.at(0, 1, p, 1), near_y)
            self.x_send(1)

        def y_last(self):
            self.yh[0].wait_recv()
            self.yh[1].wait_recv()
            self.x_send(2)

        def x_send(self, dy, src=None):
            src = self.at(0, dy, p) if src is None else src
            for d, to in ((-1, right), (1, left)):
                self.x[d, dy] = send(src, self.at(0, dy, p), to)

        def x_forward(self, dy):
            self.x[-1, dy].wait_recv()
            if dy and self.by_y:
                self.x[1, dy].wait_recv()
                return
            self.xh[0, dy] = send(self.at(-1, dy, p, 0), self.at(-1, dy, p, 0), right)
            self.x[1, dy].wait_recv()
            self.xh[1, dy] = send(self.at(1, dy, p, 1), self.at(1, dy, p, 1), left)

        def far_own(self):
            if not self.by_y:
                return
            for made in self.xh.values():
                made.wait_recv()
            self.far = {d: send(self.at(2, 0, p), self.at(2, 0, p), to) for d, to in ((-1, far_y), (1, near_y))}

        def far_forward(self):
            if not self.by_y:
                return
            self.far[-1].wait_recv()
            self.fh[0] = send(self.at(2, -1, p, 0), self.at(2, -1, p, 0), far_y)
            self.far[1].wait_recv()
            self.fh[1] = send(self.at(2, 1, p, 1), self.at(2, 1, p, 1), near_y)

        def far_last(self):
            for made in (self.fh if self.by_y else self.xh).values():
                made.wait_recv()

        def share(self, dx):
            self.sib[dx] = send(self.group(dx, p), self.group(dx, p), sibling)

    first, second = Gather(w1, w1_group, False), Gather(w2, w2_group, False)

    own_w1 = pltpu.make_async_copy(win_ref, w1(0, 0, p), local_sem.at[0])
    own_tok = pltpu.make_async_copy(tok_ref, tokp.at[yl], local_sem.at[1])
    own_w1.start()
    own_tok.start()

    barrier = pltpu.get_barrier_semaphore()
    greeted = [right, left, far_y, near_y, up, down, up_pair, down_pair, pair, sibling, spread_from, lift_from]
    for to in greeted:
        pl.semaphore_signal(barrier, inc=1, device_id=to, device_id_type=MESH)
    pl.semaphore_wait(barrier, len(greeted))

    tok_pair = send(tok_ref, tokp.at[yl], pair)
    first.x_send(0, win_ref)
    sent(tok_pair)
    first.y_own(win_ref)

    tok_pair.wait_recv()
    own_tok.wait()
    tk[z] = tokp[...].reshape(384, 256).T
    ring = {}

    def ring_step(step, halves=(0, 1)):
        for half in halves:
            for way, to in ((0, up), (1, down)):
                if step:
                    if step == 3 and half != way:
                        continue
                    ring[way, half, step - 1].wait_recv()
                at = tk.at[(z + 8 - step) % 8 if way == 0 else (z + step) % 8, pl.ds(128 * half, 128)]
                ring[way, half, step] = send(at, at, to)

    ring_step(0)
    spreading, spread_end = send_maybe(wout_ref, stage, spread)
    first.x_forward(0)
    ring_step(1)
    first.y_forward()
    spreading.wait_recv()
    lifting, lift_end = send_maybe(stage, wo.at[z, p, yh % 2], lift)
    ring_step(2)
    first.y_last()
    first.far_own()
    own_w1.wait()
    first.share(0)
    first.x_forward(-1)
    first.x_forward(1)
    ring_step(3)
    lifting.wait_recv()
    second.y_own(w2(0, 0, p))
    second.x_send(0)
    first.far_forward()
    first.x_forward(2)
    first.share(-1)
    first.share(1)
    ring[0, 0, 3].wait_recv()
    ring[1, 1, 3].wait_recv()
    ring[0, 1, 2].wait_recv()
    ring[1, 0, 2].wait_recv()

    def product(dx):
        first.sib[dx].wait_recv()
        total = None
        for k in range(2):
            at = 2 * ((x + dx) % 4) + k
            new = jnp.dot(tk[at], wi[at].reshape(384, 768), preferred_element_type=F32)
            total = new if total is None else total + new
        return total

    acc[...] = product(0)
    second.x_forward(0)
    acc[...] += product(-1)
    second.y_forward()
    acc[...] += product(1)
    first.far_last()
    first.share(2)
    second.y_last()
    second.far_own()
    second.share(0)
    acc[...] += product(2)

    @pl.loop(0, 16)
    def _(i):
        rows = pl.ds(pl.multiple_of(i * 16, 16), 16)
        hid[rows] = gelu(acc[rows]).astype(BF16)

    second.x_forward(-1)
    second.x_forward(1)
    second.far_forward()
    second.x_forward(2)
    second.share(-1)
    second.share(1)
    second.far_last()
    second.share(2)
    for dx in (0, -1, 1, 2):
        second.sib[dx].wait_recv()

    place = {4: 0, 3: 1, -3: 2, 2: 3, -2: 4, 1: 5, -1: 6, 0: 7}

    def partial(distance):
        at = (z + 8 + distance) % 8
        weights = jnp.concatenate([wo[at, 0].reshape(384, 384), wo[at, 1].reshape(384, 384)], axis=1)
        value = lax.dot_general(weights, hid[...], (((1,), (1,)), ((), ())), preferred_element_type=F32)
        part[place[distance]] = value.reshape(2, 192, 256)

    moved, swapped = {}, {}

    def swap(distance):
        slot = distance % 3
        swap_out[slot] = part[place[distance], 1 - yl].astype(BF16)
        swapped[distance] = send(swap_out.at[slot], swap_in.at[slot], pair)

    def pass_on(name, k, distance):
        for turn in range(2):
            if distance == 1 and turn == 0:
                continue
            feature = yl if turn else 1 - yl
            for way, to, cross in ((0, up, up_pair), (1, down, down_pair)):
                half = way if name == "a" else 1 - way
                lanes = slice(128 * half, 128 * half + 128)
                sign = distance if way == 0 or distance == 4 else -distance
                value = part[place[sign], feature, :, lanes]
                slot = (2 * k if name == "a" else 2 * k + 1) * 2 + turn
                if distance == 1:
                    if name == "b":
                        swapped[sign].wait_recv()
                    value = value + swap_in[sign % 3, :, lanes].astype(F32)
                    moved[way, name, k - 1, 0].wait_recv()
                    value = value + rs_in[way, slot - 5].astype(F32)
                if k:
                    moved[way, name, k - 1, turn].wait_recv()
                    value = value + rs_in[way, slot - 4].astype(F32)
                rs_out[way, slot] = value.astype(BF16)
                to = cross if distance == 2 and turn == 0 else to
                moved[way, name, k, turn] = send(rs_out.at[way, slot], rs_in.at[way, slot], to)

    partial(4)
    pass_on("a", 0, 4)
    partial(3)
    partial(-3)
    pass_on("b", 0, 3)
    partial(1)
    swap(1)
    partial(-1)
    swap(-1)
    partial(2)
    partial(-2)
    pass_on("a", 1, 3)
    pass_on("b", 1, 2)
    partial(0)
    swap(0)
    pass_on("a", 2, 2)
    old = len(started)
    pass_on("b", 2, 1)
    pass_on("a", 3, 1)
    fresh = len(started) - old
    while len(started) > fresh:
        sent(started[0])
    spread_end()
    lift_end()
    swapped[0].wait_recv()
    mine = [part[place[0], yl, :, 128 * half : 128 * half + 128] for half in range(2)]
    mine = [mine[half] + swap_in[0, :, 128 * half : 128 * half + 128].astype(F32) for half in range(2)]
    for half in range(2):
        moved[1 - half, "b", 2, 1].wait_recv()
        mine[half] = mine[half] + rs_in[1 - half, 11].astype(F32)
    for half in range(2):
        moved[half, "a", 3, 1].wait_recv()
        value = mine[half] + rs_in[half, 13].astype(F32)
        out_ref[:, 128 * half : 128 * half + 128] = value.astype(BF16)

    for made in started:
        made.wait_send()


def local(tokens, w_in, w_out):
    out = pl.pallas_call(
        kernel,
        name="mlp_block",
        out_shape=jax.ShapeDtypeStruct((192, 256), BF16),
        in_specs=[pl.BlockSpec(memory_space=pltpu.HBM)] * 3,
        out_specs=pl.BlockSpec(memory_space=pltpu.VMEM),
        scratch_shapes=[
            pltpu.VMEM((8, 256, 384), BF16),
            pltpu.VMEM((8, 2, 2, 96, 768), BF16),
            pltpu.VMEM((8, 2, 2, 192, 384), BF16),
            pltpu.VMEM((2, 192, 256), BF16),
            pltpu.VMEM((192, 384), BF16),
            pltpu.VMEM((256, 768), BF16),
            pltpu.VMEM((256, 768), F32),
            pltpu.VMEM((8, 2, 192, 256), F32),
            pltpu.VMEM((2, 14, 192, 128), BF16),
            pltpu.VMEM((2, 14, 192, 128), BF16),
            pltpu.VMEM((3, 192, 256), BF16),
            pltpu.VMEM((3, 192, 256), BF16),
            pltpu.SemaphoreType.DMA((SEMS,)),
            pltpu.SemaphoreType.DMA((SEMS,)),
            pltpu.SemaphoreType.DMA((2,)),
        ],
        compiler_params=pltpu.CompilerParams(collective_id=0, has_side_effects=True, vmem_limit_bytes=60 * 2**20),
        cost_estimate=pl.CostEstimate(flops=4 * 256 * 3072 * 768, bytes_accessed=2**20, transcendentals=2**18),
    )(tokens.T, w_in, w_out.T)
    return out.T


def solution(mesh):
    placed = (P("row", "col"), P("row", "col"), P("row", "col"))
    return jax.shard_map(local, mesh=mesh, in_specs=placed, out_specs=P("row", "col"), check_vma=False)
```

```python
import jax
import jax.numpy as jnp
from jax import lax
from jax.experimental import pallas as pl
from jax.experimental.pallas import tpu as pltpu
from jax.sharding import PartitionSpec as P

MESH = pl.DeviceIdType.MESH
BF16, F32 = jnp.bfloat16, jnp.float32
SEMS = 102


def horner(v, terms):
    total = jnp.full_like(v, terms[0])
    for term in terms[1:]:
        total = total * v + term
    return total


ERF_NEAR = (7.853861353153693e-5, -8.010193625184903e-4, 5.188327685732524e-3, -2.685381193529856e-2,
            1.128358514861418e-1, -3.761262582423300e-1, 1.128379165726710e0)
ERFC_MID = (2.326819970068386e-2, -1.387039388740657e-1, 3.687424674597105e-1, -5.824733027278666e-1,
            6.210004621745983e-1, -4.944515323274145e-1, 3.404879937665872e-1, -2.741127028184656e-1,
            5.638259427386472e-1)
ERFC_FAR = (-1.047766399936249e1, 1.297719955372516e1, -7.495518717768503e0, 2.921019019210786e0,
            -1.015265279202700e0, 4.218463358204948e-1, -2.820767439740514e-1, 5.641895067754075e-1)


def gelu(v):
    u = v * (-(0.5**0.5))
    square = u * u
    size = jnp.maximum(jnp.abs(u), 0.5)
    near = 1.0 - u * horner(jnp.minimum(square, 1.0), ERF_NEAR)
    inverse = 1.0 / size
    y = inverse * inverse
    series = jnp.where(size < 2.0, horner(jnp.minimum(y, 1.0), ERFC_MID), horner(jnp.minimum(y, 0.25), ERFC_FAR))
    tail = jnp.exp(-square) * inverse * series
    far = jnp.where(u < 0.0, 2.0 - tail, tail)
    return 0.5 * v * jnp.where(jnp.abs(u) < 1.0, near, far)


def kernel(tok_ref, win_ref, wout_ref, out_ref, tk, wi, wo, tokp, stage, hid, acc, part, rs_out, rs_in, swap_out, swap_in,
           send_sem, recv_sem, local_sem):
    r, c = lax.axis_index("row"), lax.axis_index("col")
    x, yh, p, z, yl = r // 8, (r // 2) % 4, r % 2, c // 2, c % 2

    def device(x, yh, p, z, yl):
        return ((x % 4) * 8 + (yh % 4) * 2 + p, (z % 8) * 2 + yl)

    right, left = device(x + 1, yh, p, z, yl), device(x + 3, yh, p, z, yl)
    far_y, near_y = device(x, yh + 1, p, z, yl), device(x, yh + 3, p, z, yl)
    up, down = device(x, yh, p, z + 1, yl), device(x, yh, p, z + 7, yl)
    up_pair, down_pair = device(x, yh, p, z + 1, 1 - yl), device(x, yh, p, z + 7, 1 - yl)
    pair, sibling = device(x, yh, p, z, 1 - yl), device(x, yh, 1 - p, z, yl)

    other_x = (z // 2 + 4 - x) % 4
    spread = device(other_x, 2 * ((yh // 2 + z + yl) % 2) + yl, p, z, yh % 2)
    top = (yh // 2 + z + yh) % 2
    spread_from = device(other_x, 2 * top + yl, p, z, yh % 2)
    lift = device(x, yh, p, 2 * other_x + top, yl)
    lift_from = device(x, yh, p, 2 * ((z // 2 + x) % 4) + top, yl)

    sems = [0]
    started = []

    def copy(src, dst, to):
        k = sems[0]
        sems[0] += 1
        return pltpu.make_async_remote_copy(
            src_ref=src, dst_ref=dst, send_sem=send_sem.at[k], recv_sem=recv_sem.at[k], device_id=to, device_id_type=MESH
        )

    def send(src, dst, to):
        made = copy(src, dst, to)
        made.start()
        started.append(made)
        return made

    def sent(made):
        made.wait_send()
        started[:] = [other for other in started if other is not made]

    def send_maybe(src, dst, to):
        k = sems[0]
        made = copy(src, dst, to)
        here = jnp.logical_and(to[0] == r, to[1] == c)

        @pl.when(here)
        def _():
            pltpu.make_async_copy(src, dst, recv_sem.at[k]).start()

        @pl.when(jnp.logical_not(here))
        def _():
            made.start()

        def end():
            @pl.when(jnp.logical_not(here))
            def _():
                made.wait_send()

        return made, end

    def w1(dx, dy, core, half=None):
        px, py = (x + dx) % 4, (yh + dy) % 4
        at = wi.at[2 * px + py // 2, py % 2, core]
        return at if half is None else at.at[pl.ds(48 * half, 48)]

    def w1_group(dx, core):
        return wi.at[pl.ds(2 * ((x + dx) % 4), 2), :, core]

    def w2(dx, dy, core, half=None):
        px, py = (x + dx) % 4, (yh + dy) % 4
        at = wo.at[2 * ((z // 2 + px) % 4) + (z + py // 2 + py) % 2, core, py % 2]
        return at if half is None else at.at[pl.ds(96 * half, 96)]

    def w2_group(dx, core):
        return wo.at[pl.ds(2 * ((z // 2 + x + dx) % 4), 2), core]

    class Gather:
        def __init__(self, at, group, far):
            self.at, self.group, self.by_y = at, group, far
            self.x, self.xh, self.yh, self.fh, self.sib = {}, {}, {}, {}, {}

        def y_own(self, src):
            size = src.shape[0] // 2
            self.y = {}
            for first_half in range(2):
                for d, to in ((-1, far_y), (1, near_y)):
                    half = first_half if d == -1 else 1 - first_half
                    self.y[d, half] = send(src.at[pl.ds(size * half, size)], self.at(0, 0, p, half), to)

        def y_forward(self):
            self.y[-1, 0].wait_recv()
            self.yh[0] = send(self.at(0, -1, p, 0), self.at(0, -1, p, 0), far_y)
            self.x_send_half(-1, 0)
            self.y[1, 1].wait_recv()
            self.yh[1] = send(self.at(0, 1, p, 1), self.at(0, 1, p, 1), near_y)
            self.x_send_half(1, 1)
            self.y[-1, 1].wait_recv()
            self.x_send_half(-1, 1)
            self.y[1, 0].wait_recv()
            self.x_send_half(1, 0)

        def y_last(self):
            self.yh[0].wait_recv()
            self.yh[1].wait_recv()
            self.x_send(2)

        def x_send(self, dy, src=None):
            src = self.at(0, dy, p) if src is None else src
            for d, to in ((-1, right), (1, left)):
                self.x[d, dy] = send(src, self.at(0, dy, p), to)

        def x_send_half(self, dy, half):
            for d, to in ((-1, right), (1, left)):
                self.x[d, dy, half] = send(self.at(0, dy, p, half), self.at(0, dy, p, half), to)

        def x_forward(self, dy):
            for d, half, to in ((-1, 0, right), (1, 1, left)):
                (self.x[d, dy, half] if dy in (-1, 1) else self.x[d, dy]).wait_recv()
                if not (self.by_y and dy in (-1, 1)):
                    self.xh[half, dy] = send(self.at(d, dy, p, half), self.at(d, dy, p, half), to)

        def x_rest(self):
            for dy in (-1, 1):
                self.x[-1, dy, 1].wait_recv()
                self.x[1, dy, 0].wait_recv()

        def far_own(self):
            self.xh[0, 0].wait_recv()
            self.xh[1, 0].wait_recv()
            self.far = [send(self.at(2, 0, p), self.at(2, 0, p), to) for to in (far_y, near_y)]

        def far_last(self):
            for key, made in self.xh.items():
                if not (self.by_y and key[1] == 0):
                    made.wait_recv()
            if self.by_y:
                for made in self.far:
                    made.wait_recv()

        def share(self, dx):
            self.sib[dx] = send(self.group(dx, p), self.group(dx, p), sibling)

    first, second = Gather(w1, w1_group, True), Gather(w2, w2_group, False)

    own_w1 = pltpu.make_async_copy(win_ref, w1(0, 0, p), local_sem.at[0])
    own_tok = pltpu.make_async_copy(tok_ref, tokp.at[yl], local_sem.at[1])
    own_w1.start()
    own_tok.start()

    barrier = pltpu.get_barrier_semaphore()
    greeted = [right, left, far_y, near_y, up, down, up_pair, down_pair, pair, sibling, spread_from, lift_from]
    for to in greeted:
        pl.semaphore_signal(barrier, inc=1, device_id=to, device_id_type=MESH)
    pl.semaphore_wait(barrier, len(greeted))

    ring = {}

    def product(dx):
        first.sib[dx].wait_recv()
        total = None
        for k in range(2):
            at = 2 * ((x + dx) % 4) + k
            new = jnp.dot(tk[at], wi[at].reshape(384, 768), preferred_element_type=F32)
            total = new if total is None else total + new
        return total

    def ring_step(step, halves=(0, 1)):
        for half in halves:
            for way, to in ((0, up), (1, down)):
                if step:
                    if step == 3 and half != way:
                        continue
                    ring[way, half, step - 1].wait_recv()
                at = tk.at[(z + 8 - step) % 8 if way == 0 else (z + step) % 8, pl.ds(128 * half, 128)]
                ring[way, half, step] = send(at, at, to)

    def tokens_begin():
        tok_pair.wait_recv()
        own_tok.wait()
        tk[z] = tokp[...].reshape(384, 256).T
        ring_step(0)

    spreading, spread_end = send_maybe(wout_ref, stage, spread)
    first.y_own(win_ref)
    first.x_send(0, win_ref)
    first.x_forward(0)
    tok_pair = send(tok_ref, tokp.at[yl], pair)
    spreading.wait_recv()
    lifting, lift_end = send_maybe(stage, wo.at[z, p, yh % 2], lift)
    first.y_forward()
    tokens_begin()
    first.far_own()
    first.x_forward(-1)
    ring_step(1, (0,))
    lifting.wait_recv()
    second.y_own(w2(0, 0, p))
    first.y_last()
    second.x_send(0)
    ring_step(1, (1,))
    first.x_forward(1)
    own_w1.wait()
    first.share(0)
    ring_step(2, (0,))
    first.x_forward(2)
    ring_step(2, (1,))
    second.x_forward(0)
    first.x_rest()
    first.share(-1)
    first.share(1)
    second.y_forward()
    ring_step(3)
    first.far_last()
    first.share(2)
    second.y_last()
    second.share(0)
    second.x_forward(-1)
    ring[0, 0, 3].wait_recv()
    ring[1, 1, 3].wait_recv()
    ring[0, 1, 2].wait_recv()
    ring[1, 0, 2].wait_recv()

    acc[...] = product(0)
    acc[...] += product(-1)
    second.x_forward(1)
    acc[...] += product(1)
    acc[...] += product(2)
    second.x_forward(2)

    @pl.loop(0, 16)
    def _(i):
        rows = pl.ds(pl.multiple_of(i * 16, 16), 16)
        hid[rows] = gelu(acc[rows]).astype(BF16)

    second.x_rest()
    second.share(-1)
    second.share(1)
    second.far_last()
    second.share(2)
    for dx in (0, -1, 1, 2):
        second.sib[dx].wait_recv()

    place = {4: 0, 3: 1, -3: 2, 2: 3, -2: 4, 1: 5, -1: 6, 0: 7}

    def partial(distance):
        at = (z + 8 + distance) % 8
        weights = jnp.concatenate([wo[at, 0].reshape(384, 384), wo[at, 1].reshape(384, 384)], axis=1)
        value = lax.dot_general(weights, hid[...], (((1,), (1,)), ((), ())), preferred_element_type=F32)
        part[place[distance]] = value.reshape(2, 192, 256)

    moved, swapped = {}, {}

    def swap(distance):
        slot = distance % 3
        swap_out[slot] = part[place[distance], 1 - yl].astype(BF16)
        swapped[distance] = send(swap_out.at[slot], swap_in.at[slot], pair)

    def pass_on(name, k, distance):
        for turn in range(2):
            if distance == 1 and turn == 0:
                continue
            feature = yl if turn else 1 - yl
            for way, to, cross in ((0, up, up_pair), (1, down, down_pair)):
                half = way if name == "a" else 1 - way
                lanes = slice(128 * half, 128 * half + 128)
                sign = distance if way == 0 or distance == 4 else -distance
                value = part[place[sign], feature, :, lanes]
                slot = (2 * k if name == "a" else 2 * k + 1) * 2 + turn
                if distance == 1:
                    if name == "b":
                        swapped[sign].wait_recv()
                    value = value + swap_in[sign % 3, :, lanes].astype(F32)
                    moved[way, name, k - 1, 0].wait_recv()
                    value = value + rs_in[way, slot - 5].astype(F32)
                if k:
                    moved[way, name, k - 1, turn].wait_recv()
                    value = value + rs_in[way, slot - 4].astype(F32)
                rs_out[way, slot] = value.astype(BF16)
                to = cross if distance == 2 and turn == 0 else to
                moved[way, name, k, turn] = send(rs_out.at[way, slot], rs_in.at[way, slot], to)

    partial(4)
    pass_on("a", 0, 4)
    partial(3)
    partial(-3)
    pass_on("b", 0, 3)
    partial(1)
    swap(1)
    partial(-1)
    swap(-1)
    partial(2)
    partial(-2)
    pass_on("a", 1, 3)
    pass_on("b", 1, 2)
    partial(0)
    swap(0)
    pass_on("a", 2, 2)
    old = len(started)
    pass_on("b", 2, 1)
    pass_on("a", 3, 1)
    fresh = len(started) - old
    while len(started) > fresh:
        sent(started[0])
    spread_end()
    lift_end()
    swapped[0].wait_recv()
    mine = [part[place[0], yl, :, 128 * half : 128 * half + 128] for half in range(2)]
    mine = [mine[half] + swap_in[0, :, 128 * half : 128 * half + 128].astype(F32) for half in range(2)]
    for half in range(2):
        moved[1 - half, "b", 2, 1].wait_recv()
        mine[half] = mine[half] + rs_in[1 - half, 11].astype(F32)
    for half in range(2):
        moved[half, "a", 3, 1].wait_recv()
        value = mine[half] + rs_in[half, 13].astype(F32)
        out_ref[:, 128 * half : 128 * half + 128] = value.astype(BF16)

    for made in started:
        made.wait_send()


def local(tokens, w_in, w_out):
    out = pl.pallas_call(
        kernel,
        name="mlp_block",
        out_shape=pltpu.VMEM((192, 256), BF16),
        in_specs=[pl.BlockSpec(memory_space=pltpu.HBM)] * 3,
        out_specs=pl.BlockSpec(memory_space=pltpu.VMEM),
        scratch_shapes=[
            pltpu.VMEM((8, 256, 384), BF16),
            pltpu.VMEM((8, 2, 2, 96, 768), BF16),
            pltpu.VMEM((8, 2, 2, 192, 384), BF16),
            pltpu.VMEM((2, 192, 256), BF16),
            pltpu.VMEM((192, 384), BF16),
            pltpu.VMEM((256, 768), BF16),
            pltpu.VMEM((256, 768), F32),
            pltpu.VMEM((8, 2, 192, 256), F32),
            pltpu.VMEM((2, 14, 192, 128), BF16),
            pltpu.VMEM((2, 14, 192, 128), BF16),
            pltpu.VMEM((3, 192, 256), BF16),
            pltpu.VMEM((3, 192, 256), BF16),
            pltpu.SemaphoreType.DMA((SEMS,)),
            pltpu.SemaphoreType.DMA((SEMS,)),
            pltpu.SemaphoreType.DMA((2,)),
        ],
        compiler_params=pltpu.CompilerParams(collective_id=0, has_side_effects=True, vmem_limit_bytes=60 * 2**20),
        cost_estimate=pl.CostEstimate(flops=4 * 256 * 3072 * 768, bytes_accessed=2**20, transcendentals=2**18),
    )(tokens.T, w_in, w_out.T)
    return out.T


def solution(mesh):
    placed = (P("row", "col"), P("row", "col"), P("row", "col"))
    return jax.shard_map(local, mesh=mesh, in_specs=placed, out_specs=P("row", "col"), check_vma=False)
```

```python
import jax
import jax.numpy as jnp
from jax import lax
from jax.experimental import pallas as pl
from jax.experimental.pallas import tpu as pltpu
from jax.sharding import PartitionSpec as P

MESH = pl.DeviceIdType.MESH
BF16, F32 = jnp.bfloat16, jnp.float32
SEMS = 111
OUT_SEMS = 30
SHARED = ("first", "second", "ring", "swap", "sums")


def horner(v, terms):
    total = jnp.full_like(v, terms[0])
    for term in terms[1:]:
        total = total * v + term
    return total


ERF_NEAR = (7.853861353153693e-5, -8.010193625184903e-4, 5.188327685732524e-3, -2.685381193529856e-2,
            1.128358514861418e-1, -3.761262582423300e-1, 1.128379165726710e0)
ERFC_MID = (2.326819970068386e-2, -1.387039388740657e-1, 3.687424674597105e-1, -5.824733027278666e-1,
            6.210004621745983e-1, -4.944515323274145e-1, 3.404879937665872e-1, -2.741127028184656e-1,
            5.638259427386472e-1)
ERFC_FAR = (-1.047766399936249e1, 1.297719955372516e1, -7.495518717768503e0, 2.921019019210786e0,
            -1.015265279202700e0, 4.218463358204948e-1, -2.820767439740514e-1, 5.641895067754075e-1)


def gelu(v):
    u = v * (-(0.5**0.5))
    square = u * u
    size = jnp.maximum(jnp.abs(u), 0.5)
    near = 1.0 - u * horner(jnp.minimum(square, 1.0), ERF_NEAR)
    inverse = 1.0 / size
    y = inverse * inverse
    series = jnp.where(size < 2.0, horner(jnp.minimum(y, 1.0), ERFC_MID), horner(jnp.minimum(y, 0.25), ERFC_FAR))
    tail = jnp.exp(-square) * inverse * series
    far = jnp.where(u < 0.0, 2.0 - tail, tail)
    return 0.5 * v * jnp.where(jnp.abs(u) < 1.0, near, far)


def kernel(tok_ref, win_ref, wout_ref, out_ref, tk, wi, wo, tokp, stage, hid, acc, part, rs_out, rs_in, swap_out, swap_in,
           send_sem, recv_sem, local_sem):
    r, c = lax.axis_index("row"), lax.axis_index("col")
    x, yh, p, z, yl = r // 8, (r // 2) % 4, r % 2, c // 2, c % 2

    def device(x, yh, p, z, yl):
        return ((x % 4) * 8 + (yh % 4) * 2 + p, (z % 8) * 2 + yl)

    right, left = device(x + 1, yh, p, z, yl), device(x + 3, yh, p, z, yl)
    far_y, near_y = device(x, yh + 1, p, z, yl), device(x, yh + 3, p, z, yl)
    up, down = device(x, yh, p, z + 1, yl), device(x, yh, p, z + 7, yl)
    up_pair, down_pair = device(x, yh, p, z + 1, 1 - yl), device(x, yh, p, z + 7, 1 - yl)
    pair, sibling = device(x, yh, p, z, 1 - yl), device(x, yh, 1 - p, z, yl)

    other_x = (z // 2 + 4 - x) % 4
    spread = device(other_x, 2 * ((yh // 2 + z + yl) % 2) + yl, p, z, yh % 2)
    top = (yh // 2 + z + yh) % 2
    spread_from = device(other_x, 2 * top + yl, p, z, yh % 2)
    lift = device(x, yh, p, 2 * other_x + top, yl)
    lift_from = device(x, yh, p, 2 * ((z // 2 + x) % 4) + top, yl)

    sems = [0]
    started = []

    out_sems = [len(SHARED)]

    def copy(src, dst, to, shared=None):
        k = sems[0]
        sems[0] += 1
        if shared is None:
            j = out_sems[0]
            out_sems[0] += 1
        else:
            j = SHARED.index(shared)
        return pltpu.make_async_remote_copy(
            src_ref=src, dst_ref=dst, send_sem=send_sem.at[j], recv_sem=recv_sem.at[k], device_id=to, device_id_type=MESH
        )

    def send(src, dst, to, shared=None):
        made = copy(src, dst, to, shared)
        made.start()
        if shared is None:
            started.append(made)
        return made

    def sent_all(shared, at):
        j = SHARED.index(shared)
        pltpu.make_async_copy(at, at, send_sem.at[j]).wait()

    def sent(made):
        made.wait_send()
        started[:] = [other for other in started if other is not made]

    def send_maybe(src, dst, to):
        k = sems[0]
        made = copy(src, dst, to)
        here = jnp.logical_and(to[0] == r, to[1] == c)

        @pl.when(here)
        def _():
            pltpu.make_async_copy(src, dst, recv_sem.at[k]).start()

        @pl.when(jnp.logical_not(here))
        def _():
            made.start()

        def end():
            @pl.when(jnp.logical_not(here))
            def _():
                made.wait_send()

        return made, end

    def w1(dx, dy, core, half=None):
        px, py = (x + dx) % 4, (yh + dy) % 4
        at = wi.at[2 * px + py // 2, py % 2, core]
        return at if half is None else at.at[pl.ds(48 * half, 48)]

    def w1_group(dx, core):
        return wi.at[pl.ds(2 * ((x + dx) % 4), 2), :, core]

    def w2(dx, dy, core, half=None):
        px, py = (x + dx) % 4, (yh + dy) % 4
        at = wo.at[2 * ((z // 2 + px) % 4) + (z + py // 2 + py) % 2, core, py % 2]
        return at if half is None else at.at[pl.ds(96 * half, 96)]

    def w2_group(dx, core):
        return wo.at[pl.ds(2 * ((z // 2 + x + dx) % 4), 2), core]

    class Gather:
        def __init__(self, at, group, far):
            self.at, self.group, self.by_y = at, group, far
            self.name = "first" if far else "second"
            self.x, self.xh, self.y, self.yh, self.sib = {}, {}, {}, {}, {}

        def y_own(self, src, order=(0, 1)):
            size = src.shape[0] // 2
            for first_half in order:
                for d, to in ((-1, far_y), (1, near_y)):
                    half = first_half if d == -1 else 1 - first_half
                    name = "first" if self.by_y else None
                    self.y[d, half] = send(src.at[pl.ds(size * half, size)], self.at(0, 0, p, half), to, name)

        def y_forward(self):
            self.y[-1, 0].wait_recv()
            self.yh[0] = send(self.at(0, -1, p, 0), self.at(0, -1, p, 0), far_y)
            self.x_send_half(-1, 0)
            self.y[1, 1].wait_recv()
            self.yh[1] = send(self.at(0, 1, p, 1), self.at(0, 1, p, 1), near_y)
            self.x_send_half(1, 1)
            self.y[-1, 1].wait_recv()
            self.x_send_half(-1, 1)
            self.y[1, 0].wait_recv()
            self.x_send_half(1, 0)

        def y_last(self):
            for half in range(2):
                self.yh[half].wait_recv()
                self.x_send_half(2, half)

        def x_send(self, dy, src=None):
            src = self.at(0, dy, p) if src is None else src
            for d, to in ((-1, right), (1, left)):
                self.x[d, dy] = send(src, self.at(0, dy, p), to, self.name)

        def x_send_half(self, dy, half):
            for d, to in ((-1, right), (1, left)):
                self.x[d, dy, half] = send(self.at(0, dy, p, half), self.at(0, dy, p, half), to, self.name)

        def x_forward(self, dy):
            for d, half, to in ((-1, 0, right), (1, 1, left)):
                (self.x[d, dy, half] if dy else self.x[d, dy]).wait_recv()
                if not (self.by_y and dy in (-1, 1)):
                    self.xh[half, dy] = send(self.at(d, dy, p, half), self.at(d, dy, p, half), to)

        def x_rest(self):
            for dy in (-1, 1, 2):
                self.x[-1, dy, 1].wait_recv()
                self.x[1, dy, 0].wait_recv()

        def far_own(self):
            self.xh[0, 0].wait_recv()
            self.xh[1, 0].wait_recv()
            self.far = [send(self.at(2, 0, p), self.at(2, 0, p), to, self.name) for to in (far_y, near_y)]

        def far_last(self):
            for key, made in self.xh.items():
                if not (self.by_y and key[1] == 0):
                    made.wait_recv()
            if self.by_y:
                for made in self.far:
                    made.wait_recv()

        def share_far(self, *steps):
            for dy in steps:
                self.xh[0, dy].wait_recv()
                self.xh[1, dy].wait_recv()
                at = self.at(2, dy, p)
                self.sib[2, dy] = send(at, at, sibling, self.name)

        def share(self, dx):
            self.sib[dx] = send(self.group(dx, p), self.group(dx, p), sibling, self.name)

    first, second = Gather(w1, w1_group, True), Gather(w2, w2_group, False)

    barrier = pltpu.get_barrier_semaphore()
    greeted = [lift_from, spread_from, far_y, near_y, right, left, up, down, pair, sibling, up_pair, down_pair]
    for to in greeted:
        pl.semaphore_signal(barrier, inc=1, device_id=to, device_id_type=MESH)
    own_w1 = pltpu.make_async_copy(win_ref, w1(0, 0, p), local_sem.at[0])
    own_tok = pltpu.make_async_copy(tok_ref, tokp.at[yl], local_sem.at[1])
    own_w1.start()
    own_tok.start()
    pl.semaphore_wait(barrier, len(greeted))

    ring = {}

    def product(dx):
        first.sib[dx].wait_recv()
        total = None
        for k in range(2):
            at = 2 * ((x + dx) % 4) + k
            new = jnp.dot(tk[at], wi[at].reshape(384, 768), preferred_element_type=F32)
            total = new if total is None else total + new
        return total

    def ring_step(step, halves=(0, 1)):
        for half in halves:
            for way, to in ((0, up), (1, down)):
                if step:
                    if step == 3 and half != way:
                        continue
                    ring[way, half, step - 1].wait_recv()
                at = tk.at[(z + 8 - step) % 8 if way == 0 else (z + step) % 8, pl.ds(128 * half, 128)]
                ring[way, half, step] = send(at, at, to, "ring")

    def tokens_begin():
        tok_pair.wait_recv()
        own_tok.wait()
        tk[z] = tokp[...].reshape(384, 256).T
        ring_step(0)

    halves = [pl.ds(96 * half, 96) for half in range(2)]
    spreading = [send_maybe(wout_ref.at[rows], stage.at[rows], spread) for rows in halves]
    first.y_own(win_ref)
    first.x_send(0, win_ref)
    tok_pair = send(tok_ref, tokp.at[yl], pair)
    first.x_forward(0)
    lifting = []
    for rows, (made, _) in zip(halves, spreading):
        made.wait_recv()
        lifting.append(send_maybe(stage.at[rows], wo.at[z, p, yh % 2, rows], lift))
    first.y_forward()
    tokens_begin()
    first.x_forward(-1)
    for made, _ in lifting:
        made.wait_recv()
    second.y_own(w2(0, 0, p))
    first.y_last()
    second.x_send(0)
    ring_step(1, (0,))
    first.far_own()
    ring_step(1, (1,))
    first.x_forward(1)
    own_w1.wait()
    first.share(0)
    first.x_forward(2)
    ring_step(2, (0,))
    second.y_forward()
    ring_step(2, (1,))
    second.x_forward(0)
    first.x_rest()
    first.share(-1)
    first.share(1)
    ring_step(3)
    second.y_last()
    second.share(0)
    first.far_last()
    first.share(2)
    second.x_forward(-1)
    ring[0, 0, 3].wait_recv()
    ring[1, 1, 3].wait_recv()
    ring[0, 1, 2].wait_recv()
    ring[1, 0, 2].wait_recv()

    acc[...] = product(0)
    second.x_forward(1)
    acc[...] += product(-1)
    acc[...] += product(1)
    acc[...] += product(2)
    second.x_forward(2)

    @pl.loop(0, 16)
    def _(i):
        rows = pl.ds(pl.multiple_of(i * 16, 16), 16)
        hid[rows] = gelu(acc[rows]).astype(BF16)

    second.x_rest()
    second.share(-1)
    second.share(1)
    second.share_far(0, -1, 1, 2)
    for key in (0, -1, 1, (2, 0), (2, -1), (2, 1), (2, 2)):
        second.sib[key].wait_recv()

    place = {4: 0, 3: 1, -3: 2, 2: 3, -2: 4, 1: 5, -1: 6, 0: 7}

    def partial(distance):
        at = (z + 8 + distance) % 8
        weights = jnp.concatenate([wo[at, 0].reshape(384, 384), wo[at, 1].reshape(384, 384)], axis=1)
        value = lax.dot_general(weights, hid[...], (((1,), (1,)), ((), ())), preferred_element_type=F32)
        part[place[distance]] = value.reshape(2, 192, 256)

    moved, swapped = {}, {}

    def swap(distance):
        slot = distance % 3
        swap_out[slot] = part[place[distance], 1 - yl].astype(BF16)
        swapped[distance] = send(swap_out.at[slot], swap_in.at[slot], pair, "swap")

    def pass_on(name, k, distance):
        for turn in range(2):
            if distance == 1 and turn == 0:
                continue
            feature = yl if turn else 1 - yl
            for way, to, cross in ((0, up, up_pair), (1, down, down_pair)):
                half = way if name == "a" else 1 - way
                lanes = slice(128 * half, 128 * half + 128)
                sign = distance if way == 0 or distance == 4 else -distance
                value = part[place[sign], feature, :, lanes]
                slot = (2 * k if name == "a" else 2 * k + 1) * 2 + turn
                if distance == 1:
                    if name == "b":
                        swapped[sign].wait_recv()
                    value = value + swap_in[sign % 3, :, lanes].astype(F32)
                    moved[way, name, k - 1, 0].wait_recv()
                    value = value + rs_in[way, slot - 5].astype(F32)
                if k:
                    moved[way, name, k - 1, turn].wait_recv()
                    value = value + rs_in[way, slot - 4].astype(F32)
                rs_out[way, slot] = value.astype(BF16)
                to = cross if distance == 2 and turn == 0 else to
                moved[way, name, k, turn] = send(rs_out.at[way, slot], rs_in.at[way, slot], to, "sums")

    partial(4)
    pass_on("a", 0, 4)
    partial(3)
    partial(-3)
    pass_on("b", 0, 3)
    partial(1)
    swap(1)
    partial(-1)
    swap(-1)
    partial(2)
    partial(-2)
    pass_on("a", 1, 3)
    pass_on("b", 1, 2)
    partial(0)
    swap(0)
    pass_on("a", 2, 2)
    pass_on("b", 2, 1)
    pass_on("a", 3, 1)
    while started:
        sent(started[0])
    for _, end in spreading + lifting:
        end()
    sent_all("first", wi.at[pl.ds(0, 7)])
    sent_all("second", wo.at[pl.ds(0, 6)])
    sent_all("ring", tk.at[pl.ds(0, 7)])
    sent_all("swap", swap_out)
    swapped[0].wait_recv()
    mine = [part[place[0], yl, :, 128 * half : 128 * half + 128] for half in range(2)]
    mine = [mine[half] + swap_in[0, :, 128 * half : 128 * half + 128].astype(F32) for half in range(2)]
    for half in range(2):
        moved[1 - half, "b", 2, 1].wait_recv()
        mine[half] = mine[half] + rs_in[1 - half, 11].astype(F32)
    for half in range(2):
        moved[half, "a", 3, 1].wait_recv()
        value = mine[half] + rs_in[half, 13].astype(F32)
        out_ref[:, 128 * half : 128 * half + 128] = value.astype(BF16)

    sent_all("sums", rs_out.at[:, pl.ds(0, 12)])


def local(tokens, w_in, w_out):
    out = pl.pallas_call(
        kernel,
        name="mlp_block",
        out_shape=pltpu.VMEM((192, 256), BF16),
        in_specs=[pl.BlockSpec(memory_space=pltpu.HBM)] * 3,
        out_specs=pl.BlockSpec(memory_space=pltpu.VMEM),
        scratch_shapes=[
            pltpu.VMEM((8, 256, 384), BF16),
            pltpu.VMEM((8, 2, 2, 96, 768), BF16),
            pltpu.VMEM((8, 2, 2, 192, 384), BF16),
            pltpu.VMEM((2, 192, 256), BF16),
            pltpu.VMEM((192, 384), BF16),
            pltpu.VMEM((256, 768), BF16),
            pltpu.VMEM((256, 768), F32),
            pltpu.VMEM((8, 2, 192, 256), F32),
            pltpu.VMEM((2, 14, 192, 128), BF16),
            pltpu.VMEM((2, 14, 192, 128), BF16),
            pltpu.VMEM((3, 192, 256), BF16),
            pltpu.VMEM((3, 192, 256), BF16),
            pltpu.SemaphoreType.DMA((OUT_SEMS,)),
            pltpu.SemaphoreType.DMA((SEMS,)),
            pltpu.SemaphoreType.DMA((2,)),
        ],
        compiler_params=pltpu.CompilerParams(collective_id=0, has_side_effects=True, vmem_limit_bytes=60 * 2**20),
        cost_estimate=pl.CostEstimate(flops=4 * 256 * 3072 * 768, bytes_accessed=2**20, transcendentals=2**18),
    )(tokens.T, w_in, w_out.T)
    return out.T


def solution(mesh):
    placed = (P("row", "col"), P("row", "col"), P("row", "col"))
    return jax.shard_map(local, mesh=mesh, in_specs=placed, out_specs=P("row", "col"), check_vma=False)
```

```python
import jax
import jax.numpy as jnp
from jax import lax
from jax.experimental import pallas as pl
from jax.experimental.pallas import tpu as pltpu
from jax.sharding import PartitionSpec as P

MESH = pl.DeviceIdType.MESH
BF16, F32 = jnp.bfloat16, jnp.float32
SEMS = 111
OUT_SEMS = 30
SHARED = ("first", "second", "ring", "swap", "sums")


def horner(v, terms):
    total = jnp.full_like(v, terms[0])
    for term in terms[1:]:
        total = total * v + term
    return total


ERF_NEAR = (7.853861353153693e-5, -8.010193625184903e-4, 5.188327685732524e-3, -2.685381193529856e-2,
            1.128358514861418e-1, -3.761262582423300e-1, 1.128379165726710e0)
ERFC_MID = (2.326819970068386e-2, -1.387039388740657e-1, 3.687424674597105e-1, -5.824733027278666e-1,
            6.210004621745983e-1, -4.944515323274145e-1, 3.404879937665872e-1, -2.741127028184656e-1,
            5.638259427386472e-1)
ERFC_FAR = (-1.047766399936249e1, 1.297719955372516e1, -7.495518717768503e0, 2.921019019210786e0,
            -1.015265279202700e0, 4.218463358204948e-1, -2.820767439740514e-1, 5.641895067754075e-1)


def gelu(v):
    u = v * (-(0.5**0.5))
    square = u * u
    size = jnp.maximum(jnp.abs(u), 0.5)
    near = 1.0 - u * horner(jnp.minimum(square, 1.0), ERF_NEAR)
    inverse = 1.0 / size
    y = inverse * inverse
    series = jnp.where(size < 2.0, horner(jnp.minimum(y, 1.0), ERFC_MID), horner(jnp.minimum(y, 0.25), ERFC_FAR))
    tail = jnp.exp(-square) * inverse * series
    far = jnp.where(u < 0.0, 2.0 - tail, tail)
    return 0.5 * v * jnp.where(jnp.abs(u) < 1.0, near, far)


def kernel(tok_ref, win_ref, wout_ref, out_ref, tk, wi, wo, tokp, stage, hid, acc, part, rs_out, rs_in, swap_out, swap_in,
           send_sem, recv_sem, local_sem):
    r, c = lax.axis_index("row"), lax.axis_index("col")
    x, yh, p, z, yl = r // 8, (r // 2) % 4, r % 2, c // 2, c % 2

    def device(x, yh, p, z, yl):
        return ((x % 4) * 8 + (yh % 4) * 2 + p, (z % 8) * 2 + yl)

    right, left = device(x + 1, yh, p, z, yl), device(x + 3, yh, p, z, yl)
    far_y, near_y = device(x, yh + 1, p, z, yl), device(x, yh + 3, p, z, yl)
    up, down = device(x, yh, p, z + 1, yl), device(x, yh, p, z + 7, yl)
    up_pair, down_pair = device(x, yh, p, z + 1, 1 - yl), device(x, yh, p, z + 7, 1 - yl)
    pair, sibling = device(x, yh, p, z, 1 - yl), device(x, yh, 1 - p, z, yl)

    other_x = (z // 2 + 4 - x) % 4
    spread = device(other_x, 2 * ((yh // 2 + z + yl) % 2) + yl, p, z, yh % 2)
    top = (yh // 2 + z + yh) % 2
    spread_from = device(other_x, 2 * top + yl, p, z, yh % 2)
    lift = device(x, yh, p, 2 * other_x + top, yl)
    lift_from = device(x, yh, p, 2 * ((z // 2 + x) % 4) + top, yl)

    sems = [0]
    started = []

    out_sems = [len(SHARED)]

    def copy(src, dst, to, shared=None):
        k = sems[0]
        sems[0] += 1
        if shared is None:
            j = out_sems[0]
            out_sems[0] += 1
        else:
            j = SHARED.index(shared)
        return pltpu.make_async_remote_copy(
            src_ref=src, dst_ref=dst, send_sem=send_sem.at[j], recv_sem=recv_sem.at[k], device_id=to, device_id_type=MESH
        )

    def send(src, dst, to, shared=None):
        made = copy(src, dst, to, shared)
        made.start()
        if shared is None:
            started.append(made)
        return made

    def sent_all(shared, at):
        j = SHARED.index(shared)
        pltpu.make_async_copy(at, at, send_sem.at[j]).wait()

    def sent(made):
        made.wait_send()
        started[:] = [other for other in started if other is not made]

    def send_maybe(src, dst, to):
        k = sems[0]
        made = copy(src, dst, to)
        here = jnp.logical_and(to[0] == r, to[1] == c)

        @pl.when(here)
        def _():
            pltpu.make_async_copy(src, dst, recv_sem.at[k]).start()

        @pl.when(jnp.logical_not(here))
        def _():
            made.start()

        def end():
            @pl.when(jnp.logical_not(here))
            def _():
                made.wait_send()

        return made, end

    def w1(dx, dy, core, half=None):
        px, py = (x + dx) % 4, (yh + dy) % 4
        at = wi.at[2 * px + py // 2, py % 2, core]
        return at if half is None else at.at[pl.ds(48 * half, 48)]

    def w1_group(dx, core):
        return wi.at[pl.ds(2 * ((x + dx) % 4), 2), :, core]

    def w2(dx, dy, core, half=None):
        px, py = (x + dx) % 4, (yh + dy) % 4
        at = wo.at[2 * ((z // 2 + px) % 4) + (z + py // 2 + py) % 2, core, py % 2]
        return at if half is None else at.at[pl.ds(96 * half, 96)]

    def w2_group(dx, core):
        return wo.at[pl.ds(2 * ((z // 2 + x + dx) % 4), 2), core]

    class Gather:
        def __init__(self, at, group, far):
            self.at, self.group, self.by_y = at, group, far
            self.name = "first" if far else "second"
            self.x, self.xh, self.y, self.yh, self.sib = {}, {}, {}, {}, {}

        def y_own(self, src, order=(0, 1)):
            size = src.shape[0] // 2
            for first_half in order:
                for d, to in ((-1, far_y), (1, near_y)):
                    half = first_half if d == -1 else 1 - first_half
                    name = "first" if self.by_y else None
                    self.y[d, half] = send(src.at[pl.ds(size * half, size)], self.at(0, 0, p, half), to, name)

        def y_forward(self):
            self.y[-1, 0].wait_recv()
            self.yh[0] = send(self.at(0, -1, p, 0), self.at(0, -1, p, 0), far_y)
            self.x_send_half(-1, 0)
            self.y[1, 1].wait_recv()
            self.yh[1] = send(self.at(0, 1, p, 1), self.at(0, 1, p, 1), near_y)
            self.x_send_half(1, 1)
            self.y[-1, 1].wait_recv()
            self.x_send_half(-1, 1)
            self.y[1, 0].wait_recv()
            self.x_send_half(1, 0)

        def y_last(self):
            for half in range(2):
                self.yh[half].wait_recv()
                self.x_send_half(2, half)

        def x_send(self, dy, src=None):
            src = self.at(0, dy, p) if src is None else src
            for d, to in ((-1, right), (1, left)):
                self.x[d, dy] = send(src, self.at(0, dy, p), to, self.name)

        def x_send_half(self, dy, half):
            for d, to in ((-1, right), (1, left)):
                self.x[d, dy, half] = send(self.at(0, dy, p, half), self.at(0, dy, p, half), to, self.name)

        def x_forward(self, dy):
            for d, half, to in ((-1, 0, right), (1, 1, left)):
                (self.x[d, dy, half] if dy else self.x[d, dy]).wait_recv()
                if not (self.by_y and dy in (-1, 1)):
                    self.xh[half, dy] = send(self.at(d, dy, p, half), self.at(d, dy, p, half), to)

        def x_rest(self):
            for dy in (-1, 1, 2):
                self.x[-1, dy, 1].wait_recv()
                self.x[1, dy, 0].wait_recv()

        def far_own(self):
            self.xh[0, 0].wait_recv()
            self.xh[1, 0].wait_recv()
            self.far = [send(self.at(2, 0, p), self.at(2, 0, p), to, self.name) for to in (far_y, near_y)]

        def far_last(self):
            for key, made in self.xh.items():
                if not (self.by_y and key[1] == 0):
                    made.wait_recv()
            if self.by_y:
                for made in self.far:
                    made.wait_recv()

        def share_far(self, *steps):
            for dy in steps:
                self.xh[0, dy].wait_recv()
                self.xh[1, dy].wait_recv()
                at = self.at(2, dy, p)
                self.sib[2, dy] = send(at, at, sibling, self.name)

        def share(self, dx):
            self.sib[dx] = send(self.group(dx, p), self.group(dx, p), sibling, self.name)

    first, second = Gather(w1, w1_group, True), Gather(w2, w2_group, False)

    barrier = pltpu.get_barrier_semaphore()
    greeted = [lift_from, spread_from, far_y, near_y, right, left, up, down, pair, sibling, up_pair, down_pair]
    for to in greeted:
        pl.semaphore_signal(barrier, inc=1, device_id=to, device_id_type=MESH)
    own_w1 = pltpu.make_async_copy(win_ref, w1(0, 0, p), local_sem.at[0])
    own_tok = pltpu.make_async_copy(tok_ref, tokp.at[yl], local_sem.at[1])
    own_w1.start()
    own_tok.start()
    pl.semaphore_wait(barrier, len(greeted))

    ring = {}

    def product(dx):
        first.sib[dx].wait_recv()
        total = None
        for k in range(2):
            at = 2 * ((x + dx) % 4) + k
            new = jnp.dot(tk[at], wi[at].reshape(384, 768), preferred_element_type=F32)
            total = new if total is None else total + new
        return total

    def ring_step(step, halves=(0, 1)):
        for half in halves:
            for way, to in ((0, up), (1, down)):
                if step:
                    if step == 3 and half != way:
                        continue
                    ring[way, half, step - 1].wait_recv()
                at = tk.at[(z + 8 - step) % 8 if way == 0 else (z + step) % 8, pl.ds(128 * half, 128)]
                ring[way, half, step] = send(at, at, to, "ring")

    def tokens_begin():
        tok_pair.wait_recv()
        own_tok.wait()
        tk[z] = tokp[...].reshape(384, 256).T
        ring_step(0)

    halves = [pl.ds(96 * half, 96) for half in range(2)]
    spreading = [send_maybe(wout_ref.at[rows], stage.at[rows], spread) for rows in halves]
    first.y_own(win_ref)
    first.x_send(0, win_ref)
    tok_pair = send(tok_ref, tokp.at[yl], pair)
    first.x_forward(0)
    lifting = []
    for rows, (made, _) in zip(halves, spreading):
        made.wait_recv()
        lifting.append(send_maybe(stage.at[rows], wo.at[z, p, yh % 2, rows], lift))
    first.y_forward()
    tokens_begin()
    first.x_forward(-1)
    for made, _ in lifting:
        made.wait_recv()
    second.y_own(w2(0, 0, p))
    first.y_last()
    second.x_send(0)
    ring_step(1, (0,))
    first.far_own()
    ring_step(1, (1,))
    first.x_forward(1)
    own_w1.wait()
    first.share(0)
    first.x_forward(2)
    ring_step(2, (0,))
    second.y_forward()
    ring_step(2, (1,))
    second.x_forward(0)
    first.x_rest()
    first.share(-1)
    first.share(1)
    ring_step(3)
    second.y_last()
    second.share(0)
    first.far_last()
    first.share(2)
    second.x_forward(-1)
    ring[0, 0, 3].wait_recv()
    ring[1, 1, 3].wait_recv()
    ring[0, 1, 2].wait_recv()
    ring[1, 0, 2].wait_recv()

    acc[...] = product(0)
    second.x_forward(1)
    acc[...] += product(-1)
    acc[...] += product(1)
    acc[...] += product(2)
    second.x_forward(2)
    second.x_rest()
    second.share(-1)
    second.share(1)

    @pl.loop(0, 16)
    def _(i):
        rows = pl.ds(pl.multiple_of(i * 16, 16), 16)
        hid[rows] = gelu(acc[rows]).astype(BF16)

    second.share_far(0, -1, 1, 2)
    for key in (0, -1, 1, (2, 0), (2, -1), (2, 1), (2, 2)):
        second.sib[key].wait_recv()

    place = {4: 0, 3: 1, -3: 2, 2: 3, -2: 4, 1: 5, -1: 6, 0: 7}

    def partial(distance):
        at = (z + 8 + distance) % 8
        weights = jnp.concatenate([wo[at, 0].reshape(384, 384), wo[at, 1].reshape(384, 384)], axis=1)
        value = lax.dot_general(weights, hid[...], (((1,), (1,)), ((), ())), preferred_element_type=F32)
        part[place[distance]] = value.reshape(2, 192, 256)

    moved, swapped = {}, {}

    def swap(distance):
        slot = distance % 3
        swap_out[slot] = part[place[distance], 1 - yl].astype(BF16)
        swapped[distance] = send(swap_out.at[slot], swap_in.at[slot], pair, "swap")

    def pass_on(name, k, distance):
        for turn in range(2):
            if distance == 1 and turn == 0:
                continue
            feature = yl if turn else 1 - yl
            for way, to, cross in ((0, up, up_pair), (1, down, down_pair)):
                half = way if name == "a" else 1 - way
                lanes = slice(128 * half, 128 * half + 128)
                sign = distance if way == 0 or distance == 4 else -distance
                value = part[place[sign], feature, :, lanes]
                slot = (2 * k if name == "a" else 2 * k + 1) * 2 + turn
                if distance == 1:
                    if name == "b":
                        swapped[sign].wait_recv()
                    value = value + swap_in[sign % 3, :, lanes].astype(F32)
                    moved[way, name, k - 1, 0].wait_recv()
                    value = value + rs_in[way, slot - 5].astype(F32)
                if k:
                    moved[way, name, k - 1, turn].wait_recv()
                    value = value + rs_in[way, slot - 4].astype(F32)
                rs_out[way, slot] = value.astype(BF16)
                to = cross if distance == 2 and turn == 0 else to
                moved[way, name, k, turn] = send(rs_out.at[way, slot], rs_in.at[way, slot], to, "sums")

    partial(4)
    pass_on("a", 0, 4)
    partial(3)
    partial(-3)
    pass_on("b", 0, 3)
    partial(1)
    swap(1)
    partial(-1)
    swap(-1)
    partial(2)
    partial(-2)
    pass_on("a", 1, 3)
    pass_on("b", 1, 2)
    partial(0)
    swap(0)
    pass_on("a", 2, 2)
    pass_on("b", 2, 1)
    pass_on("a", 3, 1)
    while started:
        sent(started[0])
    for _, end in spreading + lifting:
        end()
    sent_all("first", wi.at[pl.ds(0, 7)])
    sent_all("second", wo.at[pl.ds(0, 6)])
    sent_all("ring", tk.at[pl.ds(0, 7)])
    sent_all("swap", swap_out)
    swapped[0].wait_recv()
    mine = [part[place[0], yl, :, 128 * half : 128 * half + 128] for half in range(2)]
    mine = [mine[half] + swap_in[0, :, 128 * half : 128 * half + 128].astype(F32) for half in range(2)]
    for half in range(2):
        moved[1 - half, "b", 2, 1].wait_recv()
        mine[half] = mine[half] + rs_in[1 - half, 11].astype(F32)
    for half in range(2):
        moved[half, "a", 3, 1].wait_recv()
        value = mine[half] + rs_in[half, 13].astype(F32)
        out_ref[:, 128 * half : 128 * half + 128] = value.astype(BF16)

    sent_all("sums", rs_out.at[:, pl.ds(0, 12)])


def local(tokens, w_in, w_out):
    out = pl.pallas_call(
        kernel,
        name="mlp_block",
        out_shape=pltpu.VMEM((192, 256), BF16),
        in_specs=[pl.BlockSpec(memory_space=pltpu.HBM)] * 3,
        out_specs=pl.BlockSpec(memory_space=pltpu.VMEM),
        scratch_shapes=[
            pltpu.VMEM((8, 256, 384), BF16),
            pltpu.VMEM((8, 2, 2, 96, 768), BF16),
            pltpu.VMEM((8, 2, 2, 192, 384), BF16),
            pltpu.VMEM((2, 192, 256), BF16),
            pltpu.VMEM((192, 384), BF16),
            pltpu.VMEM((256, 768), BF16),
            pltpu.VMEM((256, 768), F32),
            pltpu.VMEM((8, 2, 192, 256), F32),
            pltpu.VMEM((2, 14, 192, 128), BF16),
            pltpu.VMEM((2, 14, 192, 128), BF16),
            pltpu.VMEM((3, 192, 256), BF16),
            pltpu.VMEM((3, 192, 256), BF16),
            pltpu.SemaphoreType.DMA((OUT_SEMS,)),
            pltpu.SemaphoreType.DMA((SEMS,)),
            pltpu.SemaphoreType.DMA((2,)),
        ],
        compiler_params=pltpu.CompilerParams(collective_id=0, has_side_effects=True, vmem_limit_bytes=60 * 2**20),
        cost_estimate=pl.CostEstimate(flops=4 * 256 * 3072 * 768, bytes_accessed=2**20, transcendentals=2**18),
    )(tokens.T, w_in, w_out.T)
    return out.T


def solution(mesh):
    placed = (P("row", "col"), P("row", "col"), P("row", "col"))
    return jax.shard_map(local, mesh=mesh, in_specs=placed, out_specs=P("row", "col"), check_vma=False)
```

```python
import jax
import jax.numpy as jnp
from jax import lax
from jax.experimental import pallas as pl
from jax.experimental.pallas import tpu as pltpu
from jax.sharding import PartitionSpec as P

MESH = pl.DeviceIdType.MESH
BF16, F32 = jnp.bfloat16, jnp.float32
SEMS = 111
OUT_SEMS = 30
SHARED = ("first", "second", "ring", "swap", "sums")


def horner(v, terms):
    total = jnp.full_like(v, terms[0])
    for term in terms[1:]:
        total = total * v + term
    return total


ERF_NEAR = (7.853861353153693e-5, -8.010193625184903e-4, 5.188327685732524e-3, -2.685381193529856e-2,
            1.128358514861418e-1, -3.761262582423300e-1, 1.128379165726710e0)
ERFC_MID = (2.326819970068386e-2, -1.387039388740657e-1, 3.687424674597105e-1, -5.824733027278666e-1,
            6.210004621745983e-1, -4.944515323274145e-1, 3.404879937665872e-1, -2.741127028184656e-1,
            5.638259427386472e-1)
ERFC_FAR = (-1.047766399936249e1, 1.297719955372516e1, -7.495518717768503e0, 2.921019019210786e0,
            -1.015265279202700e0, 4.218463358204948e-1, -2.820767439740514e-1, 5.641895067754075e-1)


def gelu(v):
    u = v * (-(0.5**0.5))
    square = u * u
    size = jnp.maximum(jnp.abs(u), 0.5)
    near = 1.0 - u * horner(jnp.minimum(square, 1.0), ERF_NEAR)
    inverse = 1.0 / size
    y = inverse * inverse
    series = jnp.where(size < 2.0, horner(jnp.minimum(y, 1.0), ERFC_MID), horner(jnp.minimum(y, 0.25), ERFC_FAR))
    tail = jnp.exp(-square) * inverse * series
    far = jnp.where(u < 0.0, 2.0 - tail, tail)
    return 0.5 * v * jnp.where(jnp.abs(u) < 1.0, near, far)


def kernel(tok_ref, win_ref, wout_ref, out_ref, tk, wi, wo, tokp, stage, hid, acc, part, rs_out, rs_in, swap_out, swap_in,
           send_sem, recv_sem, local_sem):
    r, c = lax.axis_index("row"), lax.axis_index("col")
    x, yh, p, z, yl = r // 8, (r // 2) % 4, r % 2, c // 2, c % 2

    def device(x, yh, p, z, yl):
        return ((x % 4) * 8 + (yh % 4) * 2 + p, (z % 8) * 2 + yl)

    right, left = device(x + 1, yh, p, z, yl), device(x + 3, yh, p, z, yl)
    far_y, near_y = device(x, yh + 1, p, z, yl), device(x, yh + 3, p, z, yl)
    up, down = device(x, yh, p, z + 1, yl), device(x, yh, p, z + 7, yl)
    up_pair, down_pair = device(x, yh, p, z + 1, 1 - yl), device(x, yh, p, z + 7, 1 - yl)
    pair, sibling = device(x, yh, p, z, 1 - yl), device(x, yh, 1 - p, z, yl)

    other_x = (z // 2 + 4 - x) % 4
    spread = device(other_x, 2 * ((yh // 2 + z + yl) % 2) + yl, p, z, yh % 2)
    top = (yh // 2 + z + yh) % 2
    spread_from = device(other_x, 2 * top + yl, p, z, yh % 2)
    lift = device(x, yh, p, 2 * other_x + top, yl)
    lift_from = device(x, yh, p, 2 * ((z // 2 + x) % 4) + top, yl)

    sems = [0]
    started = []

    out_sems = [len(SHARED)]

    def copy(src, dst, to, shared=None):
        k = sems[0]
        sems[0] += 1
        if shared is None:
            j = out_sems[0]
            out_sems[0] += 1
        else:
            j = SHARED.index(shared)
        return pltpu.make_async_remote_copy(
            src_ref=src, dst_ref=dst, send_sem=send_sem.at[j], recv_sem=recv_sem.at[k], device_id=to, device_id_type=MESH
        )

    def send(src, dst, to, shared=None):
        made = copy(src, dst, to, shared)
        made.start()
        if shared is None:
            started.append(made)
        return made

    def sent_all(shared, at):
        j = SHARED.index(shared)
        pltpu.make_async_copy(at, at, send_sem.at[j]).wait()

    def sent(made):
        made.wait_send()
        started[:] = [other for other in started if other is not made]

    def send_maybe(src, dst, to):
        k = sems[0]
        made = copy(src, dst, to)
        here = jnp.logical_and(to[0] == r, to[1] == c)

        @pl.when(here)
        def _():
            pltpu.make_async_copy(src, dst, recv_sem.at[k]).start()

        @pl.when(jnp.logical_not(here))
        def _():
            made.start()

        def end():
            @pl.when(jnp.logical_not(here))
            def _():
                made.wait_send()

        return made, end

    def w1(dx, dy, core, half=None):
        px, py = (x + dx) % 4, (yh + dy) % 4
        at = wi.at[2 * px + py // 2, py % 2, core]
        return at if half is None else at.at[pl.ds(48 * half, 48)]

    def w1_group(dx, core):
        return wi.at[pl.ds(2 * ((x + dx) % 4), 2), :, core]

    def w2(dx, dy, core, half=None):
        px, py = (x + dx) % 4, (yh + dy) % 4
        at = wo.at[2 * ((z // 2 + px) % 4) + (z + py // 2 + py) % 2, core, py % 2]
        return at if half is None else at.at[pl.ds(96 * half, 96)]

    def w2_group(dx, core):
        return wo.at[pl.ds(2 * ((z // 2 + x + dx) % 4), 2), core]

    class Gather:
        def __init__(self, at, group, far):
            self.at, self.group, self.by_y = at, group, far
            self.name = "first" if far else "second"
            self.x, self.xh, self.y, self.yh, self.sib = {}, {}, {}, {}, {}

        def y_own(self, src, order=(0, 1)):
            size = src.shape[0] // 2
            for first_half in order:
                for d, to in ((-1, far_y), (1, near_y)):
                    half = first_half if d == -1 else 1 - first_half
                    name = "first" if self.by_y else None
                    self.y[d, half] = send(src.at[pl.ds(size * half, size)], self.at(0, 0, p, half), to, name)

        def y_forward(self):
            self.y[-1, 0].wait_recv()
            self.yh[0] = send(self.at(0, -1, p, 0), self.at(0, -1, p, 0), far_y)
            self.x_send_half(-1, 0)
            self.y[1, 1].wait_recv()
            self.yh[1] = send(self.at(0, 1, p, 1), self.at(0, 1, p, 1), near_y)
            self.x_send_half(1, 1)
            self.y[-1, 1].wait_recv()
            self.x_send_half(-1, 1)
            self.y[1, 0].wait_recv()
            self.x_send_half(1, 0)

        def y_last(self):
            for half in range(2):
                self.yh[half].wait_recv()
                self.x_send_half(2, half)

        def x_send(self, dy, src=None):
            src = self.at(0, dy, p) if src is None else src
            for d, to in ((-1, right), (1, left)):
                self.x[d, dy] = send(src, self.at(0, dy, p), to, self.name)

        def x_send_half(self, dy, half):
            for d, to in ((-1, right), (1, left)):
                self.x[d, dy, half] = send(self.at(0, dy, p, half), self.at(0, dy, p, half), to, self.name)

        def x_forward(self, dy):
            for d, half, to in ((-1, 0, right), (1, 1, left)):
                (self.x[d, dy, half] if dy else self.x[d, dy]).wait_recv()
                if not (self.by_y and dy in (-1, 1)):
                    self.xh[half, dy] = send(self.at(d, dy, p, half), self.at(d, dy, p, half), to)

        def x_rest(self):
            for dy in (-1, 1, 2):
                self.x[-1, dy, 1].wait_recv()
                self.x[1, dy, 0].wait_recv()

        def far_own(self):
            self.xh[0, 0].wait_recv()
            self.xh[1, 0].wait_recv()
            self.far = [send(self.at(2, 0, p), self.at(2, 0, p), to, self.name) for to in (far_y, near_y)]

        def far_last(self):
            for key, made in self.xh.items():
                if not (self.by_y and key[1] == 0):
                    made.wait_recv()
            if self.by_y:
                for made in self.far:
                    made.wait_recv()

        def share_far(self, *steps):
            for dy in steps:
                self.xh[0, dy].wait_recv()
                self.xh[1, dy].wait_recv()
                at = self.at(2, dy, p)
                self.sib[2, dy] = send(at, at, sibling, self.name)

        def share(self, dx):
            self.sib[dx] = send(self.group(dx, p), self.group(dx, p), sibling, self.name)

    first, second = Gather(w1, w1_group, True), Gather(w2, w2_group, False)

    barrier = pltpu.get_barrier_semaphore()
    greeted = [lift_from, spread_from, far_y, near_y, right, left, up, down, pair, sibling, up_pair, down_pair]
    for to in greeted:
        pl.semaphore_signal(barrier, inc=1, device_id=to, device_id_type=MESH)
    own_w1 = pltpu.make_async_copy(win_ref, w1(0, 0, p), local_sem.at[0])
    own_tok = pltpu.make_async_copy(tok_ref, tokp.at[yl], local_sem.at[1])
    own_w1.start()
    own_tok.start()
    pl.semaphore_wait(barrier, len(greeted))

    ring = {}

    def product(dx):
        first.sib[dx].wait_recv()
        total = None
        for k in range(2):
            at = 2 * ((x + dx) % 4) + k
            new = jnp.dot(tk[at], wi[at].reshape(384, 768), preferred_element_type=F32)
            total = new if total is None else total + new
        return total

    def ring_step(step, halves=(0, 1)):
        for half in halves:
            for way, to in ((0, up), (1, down)):
                if step:
                    if step == 3 and half != way:
                        continue
                    ring[way, half, step - 1].wait_recv()
                at = tk.at[(z + 8 - step) % 8 if way == 0 else (z + step) % 8, pl.ds(128 * half, 128)]
                ring[way, half, step] = send(at, at, to, "ring")

    def tokens_begin():
        tok_pair.wait_recv()
        own_tok.wait()
        tk[z] = tokp[...].reshape(384, 256).T
        ring_step(0)

    halves = [pl.ds(96 * half, 96) for half in range(2)]
    spreading = [send_maybe(wout_ref.at[rows], stage.at[rows], spread) for rows in halves]
    first.y_own(win_ref)
    first.x_send(0, win_ref)
    tok_pair = send(tok_ref, tokp.at[yl], pair)
    first.x_forward(0)
    lifting = []
    for rows, (made, _) in zip(halves, spreading):
        made.wait_recv()
        lifting.append(send_maybe(stage.at[rows], wo.at[z, p, yh % 2, rows], lift))
    first.y_forward()
    tokens_begin()
    first.x_forward(-1)
    for made, _ in lifting:
        made.wait_recv()
    second.y_own(w2(0, 0, p))
    first.y_last()
    second.x_send(0)
    ring_step(1, (0,))
    first.far_own()
    ring_step(1, (1,))
    first.x_forward(1)
    own_w1.wait()
    first.share(0)
    first.x_forward(2)
    ring_step(2, (0,))
    second.y_forward()
    ring_step(2, (1,))
    second.x_forward(0)
    first.x_rest()
    first.share(-1)
    first.share(1)
    ring_step(3)
    second.y_last()
    second.share(0)
    first.far_last()
    first.share(2)
    second.x_forward(-1)
    ring[0, 0, 3].wait_recv()
    ring[1, 1, 3].wait_recv()
    ring[0, 1, 2].wait_recv()
    ring[1, 0, 2].wait_recv()

    acc[...] = product(0)
    second.x_forward(1)
    acc[...] += product(-1)
    acc[...] += product(1)
    acc[...] += product(2)
    second.x_forward(2)
    second.x_rest()
    second.share(-1)
    second.share(1)
    second.share_far(0, -1)

    @pl.loop(0, 16)
    def _(i):
        rows = pl.ds(pl.multiple_of(i * 16, 16), 16)
        hid[rows] = gelu(acc[rows]).astype(BF16)

    second.share_far(1, 2)
    for key in (0, -1, 1, (2, 0), (2, -1), (2, 1), (2, 2)):
        second.sib[key].wait_recv()

    place = {4: 0, 3: 1, -3: 2, 2: 3, -2: 4, 1: 5, -1: 6, 0: 7}

    def partial(distance):
        at = (z + 8 + distance) % 8
        weights = jnp.concatenate([wo[at, 0].reshape(384, 384), wo[at, 1].reshape(384, 384)], axis=1)
        value = lax.dot_general(weights, hid[...], (((1,), (1,)), ((), ())), preferred_element_type=F32)
        part[place[distance]] = value.reshape(2, 192, 256)

    moved, swapped = {}, {}

    def swap(distance):
        slot = distance % 3
        swap_out[slot] = part[place[distance], 1 - yl].astype(BF16)
        swapped[distance] = send(swap_out.at[slot], swap_in.at[slot], pair, "swap")

    def pass_on(name, k, distance):
        for turn in range(2):
            if distance == 1 and turn == 0:
                continue
            feature = yl if turn else 1 - yl
            for way, to, cross in ((0, up, up_pair), (1, down, down_pair)):
                half = way if name == "a" else 1 - way
                lanes = slice(128 * half, 128 * half + 128)
                sign = distance if way == 0 or distance == 4 else -distance
                value = part[place[sign], feature, :, lanes]
                slot = (2 * k if name == "a" else 2 * k + 1) * 2 + turn
                if distance == 1:
                    if name == "b":
                        swapped[sign].wait_recv()
                    value = value + swap_in[sign % 3, :, lanes].astype(F32)
                    moved[way, name, k - 1, 0].wait_recv()
                    value = value + rs_in[way, slot - 5].astype(F32)
                if k:
                    moved[way, name, k - 1, turn].wait_recv()
                    value = value + rs_in[way, slot - 4].astype(F32)
                rs_out[way, slot] = value.astype(BF16)
                to = cross if distance == 2 and turn == 0 else to
                moved[way, name, k, turn] = send(rs_out.at[way, slot], rs_in.at[way, slot], to, "sums")

    partial(4)
    pass_on("a", 0, 4)
    partial(3)
    partial(-3)
    pass_on("b", 0, 3)
    partial(1)
    swap(1)
    partial(-1)
    swap(-1)
    partial(2)
    partial(-2)
    pass_on("a", 1, 3)
    pass_on("b", 1, 2)
    partial(0)
    swap(0)
    pass_on("a", 2, 2)
    pass_on("b", 2, 1)
    pass_on("a", 3, 1)
    while started:
        sent(started[0])
    for _, end in spreading + lifting:
        end()
    sent_all("first", wi.at[pl.ds(0, 7)])
    sent_all("second", wo.at[pl.ds(0, 6)])
    sent_all("ring", tk.at[pl.ds(0, 7)])
    sent_all("swap", swap_out)
    swapped[0].wait_recv()
    mine = [part[place[0], yl, :, 128 * half : 128 * half + 128] for half in range(2)]
    mine = [mine[half] + swap_in[0, :, 128 * half : 128 * half + 128].astype(F32) for half in range(2)]
    for half in range(2):
        moved[1 - half, "b", 2, 1].wait_recv()
        mine[half] = mine[half] + rs_in[1 - half, 11].astype(F32)
    for half in range(2):
        moved[half, "a", 3, 1].wait_recv()
        value = mine[half] + rs_in[half, 13].astype(F32)
        out_ref[:, 128 * half : 128 * half + 128] = value.astype(BF16)

    sent_all("sums", rs_out.at[:, pl.ds(0, 12)])


def local(tokens, w_in, w_out):
    out = pl.pallas_call(
        kernel,
        name="mlp_block",
        out_shape=pltpu.VMEM((192, 256), BF16),
        in_specs=[pl.BlockSpec(memory_space=pltpu.HBM)] * 3,
        out_specs=pl.BlockSpec(memory_space=pltpu.VMEM),
        scratch_shapes=[
            pltpu.VMEM((8, 256, 384), BF16),
            pltpu.VMEM((8, 2, 2, 96, 768), BF16),
            pltpu.VMEM((8, 2, 2, 192, 384), BF16),
            pltpu.VMEM((2, 192, 256), BF16),
            pltpu.VMEM((192, 384), BF16),
            pltpu.VMEM((256, 768), BF16),
            pltpu.VMEM((256, 768), F32),
            pltpu.VMEM((8, 2, 192, 256), F32),
            pltpu.VMEM((2, 14, 192, 128), BF16),
            pltpu.VMEM((2, 14, 192, 128), BF16),
            pltpu.VMEM((3, 192, 256), BF16),
            pltpu.VMEM((3, 192, 256), BF16),
            pltpu.SemaphoreType.DMA((OUT_SEMS,)),
            pltpu.SemaphoreType.DMA((SEMS,)),
            pltpu.SemaphoreType.DMA((2,)),
        ],
        compiler_params=pltpu.CompilerParams(collective_id=0, has_side_effects=True, vmem_limit_bytes=60 * 2**20),
        cost_estimate=pl.CostEstimate(flops=4 * 256 * 3072 * 768, bytes_accessed=2**20, transcendentals=2**18),
    )(tokens.T, w_in, w_out.T)
    return out.T


def solution(mesh):
    placed = (P("row", "col"), P("row", "col"), P("row", "col"))
    return jax.shard_map(local, mesh=mesh, in_specs=placed, out_specs=P("row", "col"), check_vma=False)
```
